32 devices in a mesh: seq: 8 (over y, x, core), chan: 4 (over z).
Axes of the slice: x: 2, y: 2, z: 4, core: 2. Of those that a mesh axis runs over, the one named last changes fastest.
Arguments:
- streams: bfloat16 [5, 2048, 8192], P(None, 'seq', 'chan'), may hold values from -6 to 6
- short_filter: bfloat16 [7, 8192], P(None, 'chan'), may hold values from -2 to 2
- long_filter: bfloat16 [128, 8192], P(None, 'chan'), may hold values from -0.5 to 0.5
- edit_table: bfloat16 [16, 8, 8192], P('seq', None, 'chan'), may hold values from -0.25 to 0.25
- edit_bias: float32 [16, 4], replicated, may hold values from -8 to 8
- seq_tiles: int32 [4], replicated, may hold values from 1 to 8, 16 in all
- seq_tenant: int32 [4], replicated, may hold values from 0 to 15
Outputs:
- edited: bfloat16 [2048, 8192], P('seq', 'chan')
The draws below stay inside these ranges and needn't reach their ends.
Inputs may be any that keep to these rules, and one draw needn't show every extreme that they name: `seq_tiles`: each sequence fills whole tiles; the sequences fill all 16 tiles in order and the longest has 8.
All inputs are finite; a program needn't handle non-finite values.
Results may differ from the reference program's by a relative error of at most 0.013.
Values may be sent and summed in bfloat16 or wider, within the bound.
A program may use at most 64 MiB of HBM per device.

```python
import math
import jax
import jax.numpy as jnp
import numpy as np
from jax import lax

D = 8192
TILE_ROWS = 128
SHORT_TAPS = 7
LONG_TAPS = 128
SEQS = 4
EDIT_RANK = 4
TENANTS = 16
TOKENS = 2048
TILES = 16


def with_ends(result, key, smallest, high):
    shape = result.shape
    index_at = [jax.random.randint(jax.random.fold_in(key, axis), (), 0, shape[axis]) for axis in range(len(shape))]
    result = result.at[tuple(index_at)].set(smallest)
    longest = shape.index(max(shape))
    index_at[longest] = (index_at[longest] + 1) % shape[longest]
    return result.at[tuple(index_at)].set(high)


def steps_of(stream_key, dims, cuts, low, top_value):
    factor_of = 1.0
    for axis_at, shards_of in cuts:
        draws = jax.random.uniform(jax.random.fold_in(jax.random.fold_in(stream_key, 6), axis_at), (shards_of,), jnp.float32, low / len(cuts), top_value / len(cuts))
        factor_of = factor_of * jnp.repeat(jnp.exp(draws), dims[axis_at] // shards_of).reshape((-1,) + (1,) * (len(dims) - 1 - axis_at))
    return factor_of


def split_up(count, total, limit, slope):
    portions = [(1 << 20) // math.isqrt(rank ** slope) + 1 for rank in range(2, count + 1)]
    rest, given = total - limit - (count - 1), [1] * (count - 1)
    while rest > 0:
        candidates = [i for i in range(count - 1) if given[i] < limit]
        pool, budget = sum([portions[i] for i in candidates]), rest
        for i in candidates:
            more = min(limit - given[i], max(1, budget * portions[i] // pool), rest)
            given[i] = given[i] + more
            rest = rest - more
    return np.array([limit] + given)


def ragged_sizes(rng, count, total, bound, skew):
    if count == 2:
        one = jax.random.randint(rng, (), max(1, total - bound), min(bound, total - 1) + 1)
        return jnp.stack([one, total - one])
    sizes = jnp.asarray(split_up(count, total, bound, skew), jnp.int32)
    twos = (count - 1) // 2
    donor, sink = sizes[1:1 + 2 * twos:2], sizes[2:2 + 2 * twos:2]
    room = jnp.minimum(donor - 1, bound - sink)
    passed = jax.random.randint(jax.random.fold_in(rng, 1), (twos,), 0, 1 << 20) % (room + 1)
    sizes = sizes.at[1:1 + 2 * twos:2].set(donor - passed).at[2:2 + 2 * twos:2].set(sink + passed)
    return sizes[jax.random.permutation(jax.random.fold_in(rng, 2), count)]


def bell_draw(stream_key, dims, deviation, bound, shards=(), held_as=jnp.bfloat16):
    entries = deviation * jax.random.normal(stream_key, dims, jnp.float32)
    if shards:
        entries = entries * steps_of(stream_key, dims, shards, -0.22, 0.18)
    return jnp.clip(entries, -bound, bound).astype(held_as)


def setup_inputs(seed: int = 0) -> dict:
    arg_keys = jax.random.split(jax.random.key(seed), 8)
    return {
        "streams": bell_draw(arg_keys[0], (5, TOKENS, D), 1.0, 6.0, ((1, 8), (2, 4))),
        "short_filter": bell_draw(arg_keys[1], (SHORT_TAPS, D), SHORT_TAPS ** -0.5, 2.0, ((1, 4),)),
        "long_filter": bell_draw(arg_keys[2], (LONG_TAPS, D), LONG_TAPS ** -0.5, 0.5, ((1, 4),)),
        "edit_table": bell_draw(arg_keys[3], (TENANTS, 2 * EDIT_RANK, D), (D // 16) ** -0.5, 0.25, ((0, 8), (2, 4))),
        "edit_bias": bell_draw(arg_keys[4], (TENANTS, EDIT_RANK), 2.0, 8.0, (), jnp.float32),
        "seq_tiles": ragged_sizes(arg_keys[5], SEQS, TILES, TILES // 2, 2).astype(jnp.int32),
        "seq_tenant": with_ends(jax.random.randint(arg_keys[6], (SEQS,), 0, TENANTS), jax.random.fold_in(arg_keys[6], 1), 0, TENANTS - 1).astype(jnp.int32),
    }


def tile_layout(seq_tiles):
    seq_ends = jnp.cumsum(seq_tiles).astype(jnp.int32)
    tile_ids = jnp.arange(TILES, dtype=jnp.int32)
    seq_of = jnp.sum((seq_ends[None, :] <= tile_ids[:, None]).astype(jnp.int32), axis=1).astype(jnp.int32)
    starts = (tile_ids == 0) | jnp.any(seq_ends[None, :] == tile_ids[:, None], axis=1)
    return seq_of, starts


def masked_conv(field, starts, taps_filter):
    width = field.shape[1]
    reach = taps_filter.shape[0]
    tiles = field.reshape(TILES, TILE_ROWS, width)
    trailing = tiles[:, TILE_ROWS - (reach - 1):, :]
    earlier = jnp.concatenate([jnp.zeros((1, reach - 1, width), field.dtype), trailing[:-1]], axis=0)
    earlier = jnp.where(starts[:, None, None], jnp.zeros_like(earlier), earlier)
    window = jnp.concatenate([earlier, tiles], axis=1)

    def add_tap(offset, total):
        rows = lax.dynamic_slice_in_dim(window, reach - 1 - offset, TILE_ROWS, 1)
        return total + rows * lax.dynamic_index_in_dim(taps_filter, offset, 0, keepdims=False)

    total = lax.fori_loop(0, reach, add_tap, jnp.zeros((TILES, TILE_ROWS, width), jnp.float32))
    return total.reshape(TILES * TILE_ROWS, width)


def reference(streams, short_filter, long_filter, edit_table, edit_bias, seq_tiles, seq_tenant):
    seq_of, starts = tile_layout(seq_tiles)
    first_gate = streams[0].astype(jnp.float32)
    first_key = streams[1].astype(jnp.float32)
    first_value = streams[2].astype(jnp.float32)
    second_gate = streams[3].astype(jnp.float32)
    second_key = streams[4].astype(jnp.float32)
    gated = (first_key * first_value).astype(jnp.bfloat16)
    short_out = masked_conv(gated.astype(jnp.float32), starts, short_filter.astype(jnp.float32))
    mixed = (first_gate * short_out).astype(jnp.bfloat16)
    carried = (second_key * mixed.astype(jnp.float32)).astype(jnp.bfloat16)
    long_out = masked_conv(carried.astype(jnp.float32), starts, long_filter.astype(jnp.float32))
    hidden = (second_gate * long_out).astype(jnp.bfloat16)
    tok_seq = jnp.repeat(seq_of, TILE_ROWS)
    seq_onehot = (tok_seq[:, None] == jnp.arange(SEQS, dtype=jnp.int32)[None, :]).astype(jnp.float32)
    chosen = edit_table[seq_tenant]
    projected = jnp.dot(hidden, chosen.reshape(SEQS * 2 * EDIT_RANK, D).T, preferred_element_type=jnp.float32)
    projected = projected.reshape(TOKENS, SEQS, 2 * EDIT_RANK)
    selected = jnp.sum(projected * seq_onehot[:, :, None], axis=1)
    bias_tok = jnp.dot(seq_onehot, edit_bias[seq_tenant], precision=lax.Precision.HIGHEST)
    coefficient = selected[:, EDIT_RANK:] - selected[:, :EDIT_RANK] + bias_tok
    spread = (seq_onehot[:, :, None] * coefficient[:, None, :]).reshape(TOKENS, SEQS * EDIT_RANK)
    rows_r = chosen[:, :EDIT_RANK, :].reshape(SEQS * EDIT_RANK, D).astype(jnp.float32)
    change = jnp.dot(spread, rows_r, precision=lax.Precision.HIGHEST)
    return (hidden.astype(jnp.float32) + change).astype(jnp.bfloat16)
```

```python
import functools

import jax
import jax.numpy as jnp
import ml_dtypes
import numpy as np
from jax import lax
from jax.experimental import pallas as pl
from jax.experimental.pallas import tpu as pltpu
from jax.sharding import PartitionSpec as P

TILE = 128
SEQS = 4
ROWS8 = 8
CHUNK = 512
LEAD = 16
BF16 = jnp.bfloat16
F32 = jnp.float32


def split_np(a):
    hi = a.astype(ml_dtypes.bfloat16)
    lo = (a - hi.astype(np.float64)).astype(ml_dtypes.bfloat16)
    return hi, lo


def transforms():
    ks = np.concatenate([np.arange(0, TILE, 2), np.arange(1, TILE, 2)])
    angle = np.pi * np.outer(ks + 0.5, np.arange(TILE)) / TILE
    hi, lo = split_np(np.concatenate([np.cos(angle), -np.sin(angle)], axis=0))
    forward = np.concatenate([hi, lo], axis=1)
    back = np.concatenate([np.cos(angle).T, -np.sin(angle).T], axis=1) / TILE
    hi, lo = split_np(back)
    return forward, np.concatenate([hi, lo], axis=0)


def halves(x):
    hi = x.astype(BF16)
    return hi, (x - hi.astype(F32)).astype(BF16)


def dot(a, b):
    return jnp.dot(a, b, preferred_element_type=F32)


def main_kernel(
    n_seq, n_chan, bits,
    streams, short_f, long_f, table, bias, tiles, tenant, fwd, inv,
    hid_out, coef_out, rows_out,
    s_buf, gwin, gsend, grecv, csend, crecv, cold, spec, hspec, hid, tfull, tlast, trecv, psend, precv,
    in_sem, out_sem, g_ss, g_rs, c_ss, c_rs, t_ss, t_rs, p_ss, p_rs,
):
    chunks = s_buf.shape[0]
    per = table.shape[0]
    phases = len(bits)
    me = lax.axis_index("seq")
    z = lax.axis_index("chan")
    after = lax.rem(me + 1, n_seq)
    before = lax.rem(me + n_seq - 1, n_seq)

    def partner(p):
        b = bits[p]
        return me + b - 2 * b * lax.rem(lax.div(me, b), 2)

    def peer(d):
        return lax.rem(z + d, n_chan)

    def cols(c):
        return pl.ds(pl.multiple_of(c * CHUNK, CHUNK), CHUNK)

    tail = pl.ds(TILE - LEAD, TILE + LEAD)
    head = pl.ds(0, TILE - LEAD)

    def load(c, part):
        rows = tail if part == 0 else head
        return pltpu.make_async_copy(
            streams.at[:, rows, cols(c)], s_buf.at[c, :, rows, :], in_sem.at[part, c]
        )

    for c in range(chunks):
        load(c, 0).start()
    for c in range(chunks):
        load(c, 1).start()

    barrier = pltpu.get_barrier_semaphore()
    greeted = [{"seq": after}, {"seq": before}]
    greeted += [{"seq": partner(p)} for p in range(phases)]
    greeted += [{"chan": peer(d)} for d in range(1, n_chan)]
    for who in greeted:
        pl.semaphore_signal(barrier, inc=1, device_id=who, device_id_type=pl.DeviceIdType.MESH)
    pl.semaphore_wait(barrier, len(greeted))

    def remote(src, dst, ss, rs, who):
        return pltpu.make_async_remote_copy(
            src_ref=src, dst_ref=dst, send_sem=ss, recv_sem=rs, device_id=who,
            device_id_type=pl.DeviceIdType.MESH,
        )

    def table_copy(p):
        src = tlast if p == phases - 1 else tfull.at[p]
        dst = trecv.at[p, pl.ds(0, 16)] if p == phases - 1 else trecv.at[p]
        return remote(src, dst, t_ss.at[p], t_rs.at[p], {"seq": partner(p)})

    def gate_copy(c):
        return remote(gsend.at[c], grecv.at[c], g_ss.at[c], g_rs.at[c], {"seq": after})

    def border_copy(c):
        return remote(csend.at[c], crecv.at[c], c_ss.at[c], c_rs.at[c], {"seq": after})

    def part_copy(i, d):
        return remote(
            psend.at[i], precv.at[i, d - 1], p_ss.at[i, d - 1], p_rs.at[i, d - 1], {"chan": peer(d)}
        )

    ends = []
    for s in range(SEQS):
        ends.append(tiles[s] if s == 0 else ends[-1] + tiles[s])

    def seq_of(tile):
        return sum(jnp.where(e <= tile, 1, 0) for e in ends)

    def joined(tile):
        hits = sum(jnp.where(e == tile, 1, 0) for e in ends) + jnp.where(tile == 0, 1, 0)
        return jnp.where(hits > 0, 0.0, 1.0).astype(F32)

    join0, join1 = joined(2 * me), joined(2 * me + 1)

    def pick_tiles(src, who):
        picked = []
        for i in range(2):
            s_of = seq_of(2 * who + i)
            total = jnp.zeros((ROWS8, src.shape[1]), F32)
            for s in range(SEQS):
                total += jnp.where(s_of == s, 1.0, 0.0).astype(F32) * src[ROWS8 * s : ROWS8 * (s + 1)]
            picked.append(total)
        return jnp.concatenate(picked, axis=0)

    for c in range(chunks):
        at = slice(c * CHUNK, (c + 1) * CHUNK)
        owned = [table[k, :, at].astype(F32) for k in range(per)]
        out = []
        for s in range(SEQS):
            total = jnp.zeros((ROWS8, CHUNK), F32)
            for k in range(per):
                total += jnp.where(tenant[s] == per * me + k, 1.0, 0.0).astype(F32) * owned[k]
            out.append(total)
        tfull[0, :, at] = jnp.concatenate(out, axis=0).astype(BF16)
    if phases > 1:
        table_copy(0).start()

    def carry(c, i, dst, lead):
        base = TILE * i
        gwin[0:LEAD] = lead
        key = s_buf[c, 1, pl.ds(base, TILE), :].astype(F32)
        val = s_buf[c, 2, pl.ds(base, TILE), :].astype(F32)
        gated = (key * val).astype(BF16)
        if i == 1:
            gsend[c] = gated[TILE - LEAD :]
            gate_copy(c).start()
        gwin[LEAD:] = gated.astype(F32)
        taps = short_f[:, cols(c)].astype(F32)
        for b in range(CHUNK // 128):
            at = slice(128 * b, 128 * (b + 1))
            total = jnp.zeros((TILE, 128), F32)
            for j in range(short_f.shape[0]):
                total += taps[j : j + 1, at] * gwin[LEAD - j : LEAD - j + TILE, at]
            gate = s_buf[c, 0, pl.ds(base, TILE), at].astype(F32)
            mixed = (gate * total).astype(BF16).astype(F32)
            key2 = s_buf[c, 4, pl.ds(base, TILE), at].astype(F32)
            dst[c, :, at] = (key2 * mixed).astype(BF16)

    def table_step(p):
        table_copy(p).wait()
        total = tfull[p].astype(F32) + trecv[p].astype(F32)
        tfull[p + 1] = total.astype(BF16)
        if p + 1 < phases - 1:
            table_copy(p + 1).start()
        else:
            tlast[...] = pick_tiles(total, partner(phases - 1)).astype(BF16)
            table_copy(phases - 1).start()

    def tail_chunk(c, _):
        load(c, 0).wait()
        near = pl.ds(TILE - LEAD, LEAD)
        lead = (s_buf[c, 1, near, :].astype(F32) * s_buf[c, 2, near, :].astype(F32)).astype(BF16)
        carry(c, 1, csend, lead.astype(F32) * join1)
        border_copy(c).start()
        return 0

    lax.fori_loop(0, chunks, tail_chunk, 0)

    if phases == 1:
        tlast[...] = pick_tiles(tfull[0].astype(F32), partner(0)).astype(BF16)
        table_copy(0).start()
    if phases > 1:
        table_step(0)

    def twice(x):
        return jnp.concatenate([x, x], axis=0)

    def transform_chunk(c, _):
        hspec[c] = dot(fwd[...], twice(long_f[:, cols(c)]))
        spec[1, c] = dot(fwd[...], twice(csend[c]))
        return 0

    lax.fori_loop(0, chunks, transform_chunk, 0)
    for p in range(1, phases - 1):
        table_step(p)

    def head_chunk(c, _):
        load(c, 1).wait()
        gate_copy(c).wait_recv()
        carry(c, 0, cold, grecv[c].astype(F32) * join0)
        spec[0, c] = dot(fwd[...], twice(cold[c]))
        return 0

    lax.fori_loop(0, chunks, head_chunk, 0)

    table_copy(phases - 1).wait()
    mine = pick_tiles(tfull[phases - 1].astype(F32), me) + trecv[phases - 1, 0:16].astype(F32)
    rows_out[...] = mine.astype(BF16)

    half, quarter = TILE, TILE // 2

    def finish(c, i, prev, join):
        pre, pim = prev[:half] * join, prev[half:] * join
        cre, cim = spec[i, c, 0:half], spec[i, c, half:]
        gre = jnp.concatenate([cre[:quarter] - pim[:quarter], cre[quarter:] + pim[quarter:]], axis=0)
        gim = jnp.concatenate([cim[:quarter] + pre[:quarter], cim[quarter:] - pre[quarter:]], axis=0)
        hre, him = hspec[c, 0:half], hspec[c, half:]
        hi, lo = halves(jnp.concatenate([hre * gre - him * gim, hre * gim + him * gre], axis=0))
        both = dot(inv[...], hi)
        long_out = both[:TILE] + both[TILE:] + dot(inv[0:TILE], lo)
        base = TILE * i
        gate = s_buf[c, 3, pl.ds(base, TILE), :].astype(F32)
        hidden = (gate * long_out).astype(BF16)
        hid[c, pl.ds(base, TILE), :] = hidden
        write(c, i).start()
        return lax.dot_general(
            rows_out[:, cols(c)], hidden, (((1,), (1,)), ((), ())), preferred_element_type=F32
        )

    def write(c, i):
        rows = pl.ds(TILE * i, TILE)
        return pltpu.make_async_copy(
            hid.at[c, rows, :], hid_out.at[rows, cols(c)], out_sem.at[i, c]
        )

    def share(i, projected):
        mine = projected[ROWS8 * i : ROWS8 * (i + 1)]
        rank = ROWS8 // 2
        delta = mine[rank:] - mine[:rank]
        psend[i] = jnp.concatenate([delta, jnp.zeros_like(delta)], axis=0)
        for d in range(1, n_chan):
            part_copy(i, d).start()

    zero = jnp.zeros((2 * ROWS8, TILE), F32)
    share(1, lax.fori_loop(0, chunks, lambda c, t: t + finish(c, 1, spec[0, c], join1), zero))

    def border_chunk(c, t):
        border_copy(c).wait_recv()
        return t + finish(c, 0, dot(fwd[...], twice(crecv[c])), join0)

    share(0, lax.fori_loop(0, chunks, border_chunk, zero))

    coef_out[...] = jnp.zeros_like(coef_out)
    row = lax.broadcasted_iota(jnp.int32, (ROWS8, TILE), 0)
    for i in (1, 0):
        s_of = seq_of(2 * me + i)
        owner = tenant[0]
        for s in range(1, SEQS):
            owner = jnp.where(s_of == s, tenant[s], owner)
        total = psend[i]
        for r in range(ROWS8 // 2):
            total += jnp.where(row == r, bias[owner, r], 0.0)
        for d in range(1, n_chan):
            part_copy(i, d).wait()
            total += precv[i, d - 1]
        coef_out[ROWS8 * i : ROWS8 * (i + 1), TILE * i : TILE * (i + 1)] = total

    def drain(c, _):
        gate_copy(c).wait_send()
        border_copy(c).wait_send()
        write(c, 0).wait()
        write(c, 1).wait()
        return 0

    lax.fori_loop(0, chunks, drain, 0)


def edit_kernel(hid, coef, rows, out):
    hi, lo = halves(coef[...])
    change = lax.dot_general(
        jnp.concatenate([hi, lo], axis=0),
        jnp.concatenate([rows[...], rows[...]], axis=0),
        (((0,), (0,)), ((), ())),
        preferred_element_type=F32,
    )
    out[...] = (hid[...].astype(F32) + change).astype(BF16)


def on_device(n_seq, n_chan, streams, short_f, long_f, table, bias, tiles, tenant):
    rows, width = streams.shape[1:]
    chunks = width // CHUNK
    bits = [1 << b for b in range(n_seq.bit_length() - 1)]
    bits = bits[2:] + bits[:1] + bits[1:2]
    phases = len(bits)
    fwd, inv = transforms()
    vmem = pl.BlockSpec(memory_space=pltpu.VMEM)
    smem = pl.BlockSpec(memory_space=pltpu.SMEM)
    hbm = pl.BlockSpec(memory_space=pl.ANY)
    dma = pltpu.SemaphoreType.DMA
    hidden, coef, picked = pl.pallas_call(
        functools.partial(main_kernel, n_seq, n_chan, bits),
        out_shape=(
            jax.ShapeDtypeStruct((rows, width), BF16),
            jax.ShapeDtypeStruct((2 * ROWS8, rows), F32),
            jax.ShapeDtypeStruct((2 * ROWS8, width), BF16),
        ),
        in_specs=[hbm, vmem, vmem, vmem, smem, smem, smem, vmem, vmem],
        out_specs=(hbm, vmem, vmem),
        scratch_shapes=[
            pltpu.VMEM((chunks, 5, rows, CHUNK), BF16),
            pltpu.VMEM((LEAD + TILE, CHUNK), F32),
            pltpu.VMEM((chunks, LEAD, CHUNK), BF16),
            pltpu.VMEM((chunks, LEAD, CHUNK), BF16),
            pltpu.VMEM((chunks, TILE, CHUNK), BF16),
            pltpu.VMEM((chunks, TILE, CHUNK), BF16),
            pltpu.VMEM((chunks, TILE, CHUNK), BF16),
            pltpu.VMEM((2, chunks, 2 * TILE, CHUNK), F32),
            pltpu.VMEM((chunks, 2 * TILE, CHUNK), F32),
            pltpu.VMEM((chunks, rows, CHUNK), BF16),
            pltpu.VMEM((phases, SEQS * ROWS8, width), BF16),
            pltpu.VMEM((2 * ROWS8, width), BF16),
            pltpu.VMEM((phases, SEQS * ROWS8, width), BF16),
            pltpu.VMEM((2, ROWS8, TILE), F32),
            pltpu.VMEM((2, n_chan - 1, ROWS8, TILE), F32),
            dma((2, chunks)),
            dma((2, chunks)),
            dma((chunks,)),
            dma((chunks,)),
            dma((chunks,)),
            dma((chunks,)),
            dma((phases,)),
            dma((phases,)),
            dma((2, n_chan - 1)),
            dma((2, n_chan - 1)),
        ],
        compiler_params=pltpu.CompilerParams(
            collective_id=0, has_side_effects=True, vmem_limit_bytes=40 * 2**20
        ),
    )(streams, short_f, long_f, table, bias, tiles, tenant, jnp.asarray(fwd), jnp.asarray(inv))
    return pl.pallas_call(
        edit_kernel,
        grid=(chunks,),
        out_shape=jax.ShapeDtypeStruct((rows, width), BF16),
        in_specs=[
            pl.BlockSpec((rows, CHUNK), lambda c: (0, c)),
            pl.BlockSpec((2 * ROWS8, rows), lambda c: (0, 0)),
            pl.BlockSpec((2 * ROWS8, CHUNK), lambda c: (0, c)),
        ],
        out_specs=pl.BlockSpec((rows, CHUNK), lambda c: (0, c)),
    )(hidden, coef, picked)


def solution(mesh):
    in_specs = (
        P(None, "seq", "chan"),
        P(None, "chan"),
        P(None, "chan"),
        P("seq", None, "chan"),
        P(),
        P(),
        P(),
    )
    body = functools.partial(on_device, mesh.shape["seq"], mesh.shape["chan"])
    return jax.shard_map(
        body, mesh=mesh, in_specs=in_specs, out_specs=P("seq", "chan"), check_vma=False
    )
```

```python
import functools

import jax
import jax.numpy as jnp
import ml_dtypes
import numpy as np
from jax import lax
from jax.experimental import pallas as pl
from jax.experimental.pallas import tpu as pltpu
from jax.sharding import PartitionSpec as P

TILE = 128
SEQS = 4
ROWS8 = 8
CHUNK = 512
LEAD = 16
BF16 = jnp.bfloat16
F32 = jnp.float32


def split_np(a):
    hi = a.astype(ml_dtypes.bfloat16)
    lo = (a - hi.astype(np.float64)).astype(ml_dtypes.bfloat16)
    return hi, lo


def transforms():
    ks = np.concatenate([np.arange(0, TILE, 2), np.arange(1, TILE, 2)])
    angle = np.pi * np.outer(ks + 0.5, np.arange(TILE)) / TILE
    hi, lo = split_np(np.concatenate([np.cos(angle), -np.sin(angle)], axis=0))
    forward = np.concatenate([hi, lo], axis=1)
    back = np.concatenate([np.cos(angle).T, -np.sin(angle).T], axis=1) / TILE
    hi, lo = split_np(back)
    return forward, np.concatenate([hi, lo], axis=0)


def halves(x):
    hi = x.astype(BF16)
    return hi, (x - hi.astype(F32)).astype(BF16)


def dot(a, b):
    return jnp.dot(a, b, preferred_element_type=F32)


def main_kernel(
    n_seq, n_chan, bits,
    streams, short_h, long_h, table_h, bias, tiles, tenant, fwd_h, inv_h,
    out,
    short_f, long_f, table, fwd, inv, rows_own,
    s_buf, gwin, gsend, grecv, csend, crecv, cold, spec, hspec, tfull, tlast, trecv, psend, precv,
    in_sem, side_sem, g_ss, g_rs, c_ss, c_rs, t_ss, t_rs, p_ss, p_rs,
):
    chunks = s_buf.shape[0]
    per = table.shape[0]
    phases = len(bits)
    me = lax.axis_index("seq")
    z = lax.axis_index("chan")
    after = lax.rem(me + 1, n_seq)
    before = lax.rem(me + n_seq - 1, n_seq)

    def partner(p):
        b = bits[p]
        return me + b - 2 * b * lax.rem(lax.div(me, b), 2)

    def peer(d):
        return lax.rem(z + d, n_chan)

    def cols(c):
        return pl.ds(pl.multiple_of(c * CHUNK, CHUNK), CHUNK)

    tail = pl.ds(TILE - LEAD, TILE + LEAD)
    head = pl.ds(0, TILE - LEAD)

    def load(c, part):
        rows = tail if part == 0 else head
        return pltpu.make_async_copy(
            streams.at[:, rows, cols(c)], s_buf.at[c, :, rows, :], in_sem.at[part, c]
        )

    sides = [
        pltpu.make_async_copy(src, dst, side_sem.at[k])
        for k, (src, dst) in enumerate(
            ((table_h, table), (short_h, short_f), (fwd_h, fwd), (long_h, long_f), (inv_h, inv))
        )
    ]
    sides[0].start()
    sides[1].start()
    for c in range(chunks):
        load(c, 0).start()
    for k in (2, 3, 4):
        sides[k].start()
    for c in range(chunks):
        load(c, 1).start()

    barrier = pltpu.get_barrier_semaphore()
    greeted = [{"seq": after}, {"seq": before}]
    greeted += [{"seq": partner(p)} for p in range(phases)]
    greeted += [{"chan": peer(d)} for d in range(1, n_chan)]
    for who in greeted:
        pl.semaphore_signal(barrier, inc=1, device_id=who, device_id_type=pl.DeviceIdType.MESH)
    pl.semaphore_wait(barrier, len(greeted))

    def remote(src, dst, ss, rs, who):
        return pltpu.make_async_remote_copy(
            src_ref=src, dst_ref=dst, send_sem=ss, recv_sem=rs, device_id=who,
            device_id_type=pl.DeviceIdType.MESH,
        )

    def table_copy(p):
        src = tlast if p == phases - 1 else tfull.at[p]
        dst = trecv.at[p, pl.ds(0, 16)] if p == phases - 1 else trecv.at[p]
        return remote(src, dst, t_ss.at[p], t_rs.at[p], {"seq": partner(p)})

    def gate_copy(c):
        return remote(gsend.at[c], grecv.at[c], g_ss.at[c], g_rs.at[c], {"seq": after})

    def border_copy(c):
        return remote(csend.at[c], crecv.at[c], c_ss.at[c], c_rs.at[c], {"seq": after})

    def part_copy(i, d):
        return remote(
            psend.at[i], precv.at[i, d - 1], p_ss.at[i, d - 1], p_rs.at[i, d - 1], {"chan": peer(d)}
        )

    ends = []
    for s in range(SEQS):
        ends.append(tiles[s] if s == 0 else ends[-1] + tiles[s])

    def seq_of(tile):
        return sum(jnp.where(e <= tile, 1, 0) for e in ends)

    def joined(tile):
        hits = sum(jnp.where(e == tile, 1, 0) for e in ends) + jnp.where(tile == 0, 1, 0)
        return jnp.where(hits > 0, 0.0, 1.0).astype(F32)

    join0, join1 = joined(2 * me), joined(2 * me + 1)

    def pick_tiles(src, who):
        picked = []
        for i in range(2):
            s_of = seq_of(2 * who + i)
            total = jnp.zeros((ROWS8, src.shape[1]), F32)
            for s in range(SEQS):
                total += jnp.where(s_of == s, 1.0, 0.0).astype(F32) * src[ROWS8 * s : ROWS8 * (s + 1)]
            picked.append(total)
        return jnp.concatenate(picked, axis=0)

    sides[0].wait()
    for c in range(chunks):
        at = slice(c * CHUNK, (c + 1) * CHUNK)
        owned = [table[k, :, at].astype(F32) for k in range(per)]
        by_seq = []
        for s in range(SEQS):
            total = jnp.zeros((ROWS8, CHUNK), F32)
            for k in range(per):
                total += jnp.where(tenant[s] == per * me + k, 1.0, 0.0).astype(F32) * owned[k]
            by_seq.append(total)
        tfull[0, :, at] = jnp.concatenate(by_seq, axis=0).astype(BF16)
    if phases > 1:
        table_copy(0).start()

    def carry(c, i, dst, lead):
        base = TILE * i
        for b in range(CHUNK // 128):
            gwin[b, 0:LEAD] = lead[:, 128 * b : 128 * (b + 1)]
        key = s_buf[c, 1, pl.ds(base, TILE), :].astype(F32)
        val = s_buf[c, 2, pl.ds(base, TILE), :].astype(F32)
        gated = (key * val).astype(BF16)
        if i == 1:
            gsend[c] = gated[TILE - LEAD :]
            gate_copy(c).start()
        for b in range(CHUNK // 128):
            gwin[b, LEAD:] = gated[:, 128 * b : 128 * (b + 1)].astype(F32)
        taps = short_f[:, cols(c)].astype(F32)
        for b in range(CHUNK // 128):
            at = slice(128 * b, 128 * (b + 1))
            total = jnp.zeros((TILE, 128), F32)
            for j in range(short_f.shape[0]):
                total += taps[j : j + 1, at] * gwin[b, LEAD - j : LEAD - j + TILE]
            gate = s_buf[c, 0, pl.ds(base, TILE), at].astype(F32)
            mixed = (gate * total).astype(BF16).astype(F32)
            key2 = s_buf[c, 4, pl.ds(base, TILE), at].astype(F32)
            dst[c, :, at] = (key2 * mixed).astype(BF16)

    def table_step(p):
        table_copy(p).wait()
        total = tfull[p].astype(F32) + trecv[p].astype(F32)
        tfull[p + 1] = total.astype(BF16)
        if p + 1 < phases - 1:
            table_copy(p + 1).start()
        else:
            tlast[...] = pick_tiles(total, partner(phases - 1)).astype(BF16)
            table_copy(phases - 1).start()

    def tail_chunk(c, _):
        load(c, 0).wait()
        near = pl.ds(TILE - LEAD, LEAD)
        lead = (s_buf[c, 1, near, :].astype(F32) * s_buf[c, 2, near, :].astype(F32)).astype(BF16)
        carry(c, 1, csend, lead.astype(F32) * join1)
        border_copy(c).start()
        return 0

    sides[1].wait()
    lax.fori_loop(0, chunks, tail_chunk, 0)

    if phases == 1:
        tlast[...] = pick_tiles(tfull[0].astype(F32), partner(0)).astype(BF16)
        table_copy(0).start()
    if phases > 1:
        table_step(0)

    def twice(x):
        return jnp.concatenate([x, x], axis=0)

    def transform_chunk(c, _):
        hspec[c] = dot(fwd[...], twice(long_f[:, cols(c)]))
        spec[1, c] = dot(fwd[...], twice(csend[c]))
        return 0

    for k in (2, 3, 4):
        sides[k].wait()
    lax.fori_loop(0, chunks, transform_chunk, 0)
    for p in range(1, phases - 1):
        table_step(p)

    def head_chunk(c, _):
        load(c, 1).wait()
        gate_copy(c).wait_recv()
        carry(c, 0, cold, grecv[c].astype(F32) * join0)
        spec[0, c] = dot(fwd[...], twice(cold[c]))
        return 0

    lax.fori_loop(0, chunks, head_chunk, 0)

    table_copy(phases - 1).wait()
    mine = pick_tiles(tfull[phases - 1].astype(F32), me) + trecv[phases - 1, 0:16].astype(F32)
    rows_own[...] = mine.astype(BF16)

    half, quarter = TILE, TILE // 2

    def finish(c, i, prev, join):
        pre, pim = prev[:half] * join, prev[half:] * join
        cre, cim = spec[i, c, 0:half], spec[i, c, half:]
        gre = jnp.concatenate([cre[:quarter] - pim[:quarter], cre[quarter:] + pim[quarter:]], axis=0)
        gim = jnp.concatenate([cim[:quarter] + pre[:quarter], cim[quarter:] - pre[quarter:]], axis=0)
        hre, him = hspec[c, 0:half], hspec[c, half:]
        hi, lo = halves(jnp.concatenate([hre * gre - him * gim, hre * gim + him * gre], axis=0))
        both = dot(inv[...], hi)
        long_out = both[:TILE] + both[TILE:] + dot(inv[0:TILE], lo)
        base = TILE * i
        gate = s_buf[c, 3, pl.ds(base, TILE), :].astype(F32)
        hidden = (gate * long_out).astype(BF16)
        out[pl.ds(base, TILE), cols(c)] = hidden
        return lax.dot_general(
            rows_own[:, cols(c)], hidden, (((1,), (1,)), ((), ())), preferred_element_type=F32
        )

    def share(i, projected):
        mine = projected[ROWS8 * i : ROWS8 * (i + 1)]
        rank = ROWS8 // 2
        delta = mine[rank:] - mine[:rank]
        psend[i] = jnp.concatenate([delta, jnp.zeros_like(delta)], axis=0)
        for d in range(1, n_chan):
            part_copy(i, d).start()

    zero = jnp.zeros((2 * ROWS8, TILE), F32)
    share(1, lax.fori_loop(0, chunks, lambda c, t: t + finish(c, 1, spec[0, c], join1), zero))

    def border_chunk(c, t):
        border_copy(c).wait_recv()
        return t + finish(c, 0, dot(fwd[...], twice(crecv[c])), join0)

    share(0, lax.fori_loop(0, chunks, border_chunk, zero))

    row = lax.broadcasted_iota(jnp.int32, (ROWS8, TILE), 0)
    for i in (1, 0):
        s_of = seq_of(2 * me + i)
        owner = tenant[0]
        for s in range(1, SEQS):
            owner = jnp.where(s_of == s, tenant[s], owner)
        total = psend[i]
        for r in range(ROWS8 // 2):
            total += jnp.where(row == r, bias[r, owner], 0.0)
        for d in range(1, n_chan):
            part_copy(i, d).wait()
            total += precv[i, d - 1]
        blank = jnp.zeros_like(total)
        total = jnp.concatenate([total, blank] if i == 0 else [blank, total], axis=0)
        hi, lo = halves(jnp.concatenate([total, jnp.zeros((TILE - 2 * ROWS8, TILE), F32)], axis=0).T)
        spread = jnp.concatenate([hi[:, : 2 * ROWS8], lo[:, : 2 * ROWS8]], axis=1)
        rows = slice(TILE * i, TILE * (i + 1))

        def edit_chunk(c, _):
            change = dot(spread, twice(rows_own[:, cols(c)]))
            out[rows, cols(c)] = (out[rows, cols(c)].astype(F32) + change).astype(BF16)
            return 0

        lax.fori_loop(0, chunks, edit_chunk, 0)

    def drain(c, _):
        gate_copy(c).wait_send()
        border_copy(c).wait_send()
        return 0

    lax.fori_loop(0, chunks, drain, 0)


def on_device(n_seq, n_chan, streams, short_f, long_f, table, bias, tiles, tenant):
    rows, width = streams.shape[1:]
    chunks = width // CHUNK
    bits = [1 << b for b in range(n_seq.bit_length() - 1)]
    bits = bits[2:] + bits[:1] + bits[1:2]
    phases = len(bits)
    fwd, inv = transforms()
    vmem = pl.BlockSpec(memory_space=pltpu.VMEM)
    smem = pl.BlockSpec(memory_space=pltpu.SMEM)
    hbm = pl.BlockSpec(memory_space=pltpu.HBM)
    dma = pltpu.SemaphoreType.DMA
    return pl.pallas_call(
        functools.partial(main_kernel, n_seq, n_chan, bits),
        out_shape=jax.ShapeDtypeStruct((rows, width), BF16),
        in_specs=[hbm, hbm, hbm, hbm, smem, smem, smem, hbm, hbm],
        out_specs=vmem,
        scratch_shapes=[
            pltpu.VMEM(short_f.shape, BF16),
            pltpu.VMEM(long_f.shape, BF16),
            pltpu.VMEM(table.shape, BF16),
            pltpu.VMEM(fwd.shape, BF16),
            pltpu.VMEM(inv.shape, BF16),
            pltpu.VMEM((2 * ROWS8, width), BF16),
            pltpu.VMEM((chunks, 5, rows, CHUNK), BF16),
            pltpu.VMEM((CHUNK // 128, LEAD + TILE, 128), F32),
            pltpu.VMEM((chunks, LEAD, CHUNK), BF16),
            pltpu.VMEM((chunks, LEAD, CHUNK), BF16),
            pltpu.VMEM((chunks, TILE, CHUNK), BF16),
            pltpu.VMEM((chunks, TILE, CHUNK), BF16),
            pltpu.VMEM((chunks, TILE, CHUNK), BF16),
            pltpu.VMEM((2, chunks, 2 * TILE, CHUNK), F32),
            pltpu.VMEM((chunks, 2 * TILE, CHUNK), F32),
            pltpu.VMEM((phases, SEQS * ROWS8, width), BF16),
            pltpu.VMEM((2 * ROWS8, width), BF16),
            pltpu.VMEM((phases, SEQS * ROWS8, width), BF16),
            pltpu.VMEM((2, ROWS8, TILE), F32),
            pltpu.VMEM((2, n_chan - 1, ROWS8, TILE), F32),
            dma((2, chunks)),
            dma((5,)),
            dma((chunks,)),
            dma((chunks,)),
            dma((chunks,)),
            dma((chunks,)),
            dma((phases,)),
            dma((phases,)),
            dma((2, n_chan - 1)),
            dma((2, n_chan - 1)),
        ],
        compiler_params=pltpu.CompilerParams(
            collective_id=0, has_side_effects=True, vmem_limit_bytes=56 * 2**20
        ),
    )(streams, short_f, long_f, table, bias.T, tiles, tenant, jnp.asarray(fwd), jnp.asarray(inv))


def solution(mesh):
    in_specs = (
        P(None, "seq", "chan"),
        P(None, "chan"),
        P(None, "chan"),
        P("seq", None, "chan"),
        P(),
        P(),
        P(),
    )
    body = functools.partial(on_device, mesh.shape["seq"], mesh.shape["chan"])
    return jax.shard_map(
        body, mesh=mesh, in_specs=in_specs, out_specs=P("seq", "chan"), check_vma=False
    )
```

```python
import functools

import jax
import jax.numpy as jnp
import ml_dtypes
import numpy as np
from jax import lax
from jax.experimental import pallas as pl
from jax.experimental.pallas import tpu as pltpu
from jax.sharding import PartitionSpec as P

TILE = 128
SEQS = 4
ROWS8 = 8
CHUNK = 512
LEAD = 16
BF16 = jnp.bfloat16
F32 = jnp.float32


def split_np(a):
    hi = a.astype(ml_dtypes.bfloat16)
    lo = (a - hi.astype(np.float64)).astype(ml_dtypes.bfloat16)
    return hi, lo


def transforms():
    ks = np.concatenate([np.arange(0, TILE, 2), np.arange(1, TILE, 2)])
    angle = np.pi * np.outer(ks + 0.5, np.arange(TILE)) / TILE
    hi, lo = split_np(np.concatenate([np.cos(angle), -np.sin(angle)], axis=0))
    forward = np.concatenate([hi, lo], axis=1)
    back = np.concatenate([np.cos(angle).T, -np.sin(angle).T], axis=1) / TILE
    hi, lo = split_np(back)
    return forward, np.concatenate([hi, lo], axis=0)


def halves(x):
    hi = x.astype(BF16)
    return hi, (x - hi.astype(F32)).astype(BF16)


def dot(a, b):
    return jnp.dot(a, b, preferred_element_type=F32)


def main_kernel(
    n_seq, n_chan,
    streams, short_h, long_h, table_h, bias, tiles, tenant, fwd_h, inv_h,
    out,
    short_f, long_f, table, fwd, inv, rows_own,
    s_buf, gwin, gsend, grecv, csend, crecv, cold, spec, hspec, tcol, tsend, trecv, psend, precv,
    in_sem, side_sem, g_ss, g_rs, c_ss, c_rs, t_ss, t_rs, p_ss, p_rs,
):
    chunks = s_buf.shape[0]
    per = table.shape[0]
    side = n_seq // 2
    me = lax.axis_index("seq")
    z = lax.axis_index("chan")
    after = lax.rem(me + 1, n_seq)
    before = lax.rem(me + n_seq - 1, n_seq)

    flip = me + 2 - 4 * lax.rem(lax.div(me, 2), 2)
    place = lax.div(me, 4) * 2 + lax.rem(me, 2)

    def beside(d):
        at = lax.rem(place + d + side, side)
        return lax.div(at, 2) * 4 + lax.rem(lax.div(me, 2), 2) * 2 + lax.rem(at, 2)

    def peer(d):
        return lax.rem(z + d, n_chan)

    def cols(c):
        return pl.ds(pl.multiple_of(c * CHUNK, CHUNK), CHUNK)

    tail = pl.ds(TILE - LEAD, TILE + LEAD)
    head = pl.ds(0, TILE - LEAD)

    def load(c, part):
        rows = tail if part == 0 else head
        return pltpu.make_async_copy(
            streams.at[:, rows, cols(c)], s_buf.at[c, :, rows, :], in_sem.at[part, c]
        )

    sides = [
        pltpu.make_async_copy(src, dst, side_sem.at[k])
        for k, (src, dst) in enumerate(
            ((table_h, table), (short_h, short_f), (fwd_h, fwd), (long_h, long_f), (inv_h, inv))
        )
    ]
    sides[0].start()
    sides[1].start()
    for c in range(chunks):
        load(c, 0).start()
    for k in (2, 3, 4):
        sides[k].start()
    for c in range(chunks):
        load(c, 1).start()

    barrier = pltpu.get_barrier_semaphore()
    greeted = [{"seq": after}, {"seq": before}]
    greeted += [{"seq": beside(d)} for d in range(1, side)] + [{"seq": flip}]
    greeted += [{"chan": peer(d)} for d in range(1, n_chan)]
    for who in greeted:
        pl.semaphore_signal(barrier, inc=1, device_id=who, device_id_type=pl.DeviceIdType.MESH)

    def remote(src, dst, ss, rs, who):
        return pltpu.make_async_remote_copy(
            src_ref=src, dst_ref=dst, send_sem=ss, recv_sem=rs, device_id=who,
            device_id_type=pl.DeviceIdType.MESH,
        )

    def table_copy(d):
        return remote(table, tcol.at[d - 1], t_ss.at[d], t_rs.at[d], {"seq": beside(d)})

    def flip_copy():
        return remote(tsend, trecv, t_ss.at[0], t_rs.at[0], {"seq": flip})

    def gate_copy(c):
        return remote(gsend.at[c], grecv.at[c], g_ss.at[c], g_rs.at[c], {"seq": after})

    def border_copy(c):
        return remote(csend.at[c], crecv.at[c], c_ss.at[c], c_rs.at[c], {"seq": after})

    def part_copy(i, d):
        return remote(
            psend.at[i], precv.at[i, d - 1], p_ss.at[i, d - 1], p_rs.at[i, d - 1], {"chan": peer(d)}
        )

    ends = []
    for s in range(SEQS):
        ends.append(tiles[s] if s == 0 else ends[-1] + tiles[s])

    def seq_of(tile):
        return sum(jnp.where(e <= tile, 1, 0) for e in ends)

    def joined(tile):
        hits = sum(jnp.where(e == tile, 1, 0) for e in ends) + jnp.where(tile == 0, 1, 0)
        return jnp.where(hits > 0, 0.0, 1.0).astype(F32)

    join0, join1 = joined(2 * me), joined(2 * me + 1)

    def pick_tiles(who, at):
        owned = [(me, table)] + [(beside(-d), tcol.at[d - 1]) for d in range(1, side)]
        picked = []
        for i in range(2):
            s_of = seq_of(2 * who + i)
            wanted = tenant[0]
            for s in range(1, SEQS):
                wanted = jnp.where(s_of == s, tenant[s], wanted)
            total = jnp.zeros((ROWS8, CHUNK), F32)
            for owner, rows in owned:
                for k in range(per):
                    factor = jnp.where(wanted == per * owner + k, 1.0, 0.0).astype(F32)
                    total += factor * rows[k, :, at].astype(F32)
            picked.append(total)
        return jnp.concatenate(picked, axis=0)

    def carry(c, i, dst, lead):
        base = TILE * i
        for b in range(CHUNK // 128):
            gwin[b, 0:LEAD] = lead[:, 128 * b : 128 * (b + 1)]
        key = s_buf[c, 1, pl.ds(base, TILE), :].astype(F32)
        val = s_buf[c, 2, pl.ds(base, TILE), :].astype(F32)
        gated = (key * val).astype(BF16)
        if i == 1:
            gsend[c] = gated[TILE - LEAD :]
        for b in range(CHUNK // 128):
            gwin[b, LEAD:] = gated[:, 128 * b : 128 * (b + 1)].astype(F32)
        taps = short_f[:, cols(c)].astype(F32)
        for b in range(CHUNK // 128):
            at = slice(128 * b, 128 * (b + 1))
            total = jnp.zeros((TILE, 128), F32)
            for j in range(short_f.shape[0]):
                total += taps[j : j + 1, at] * gwin[b, LEAD - j : LEAD - j + TILE]
            gate = s_buf[c, 0, pl.ds(base, TILE), at].astype(F32)
            mixed = (gate * total).astype(BF16).astype(F32)
            key2 = s_buf[c, 4, pl.ds(base, TILE), at].astype(F32)
            dst[c, :, at] = (key2 * mixed).astype(BF16)

    def tail_chunk(c, _):
        load(c, 0).wait()
        near = pl.ds(TILE - LEAD, LEAD)
        lead = (s_buf[c, 1, near, :].astype(F32) * s_buf[c, 2, near, :].astype(F32)).astype(BF16)
        carry(c, 1, csend, lead.astype(F32) * join1)
        return 0

    sides[1].wait()
    lax.fori_loop(0, chunks, tail_chunk, 0)

    def twice(x):
        return jnp.concatenate([x, x], axis=0)

    def filter_chunk(c, _):
        hspec[c] = dot(fwd[...], twice(long_f[:, cols(c)]))
        return 0

    for k in (0, 2, 3, 4):
        sides[k].wait()
    lax.fori_loop(0, chunks, filter_chunk, 0)

    pl.semaphore_wait(barrier, len(greeted))
    for c in range(chunks):
        gate_copy(c).start()
    for d in range(1, side):
        table_copy(d).start()
    for c in range(chunks):
        border_copy(c).start()

    def transform_chunk(c, _):
        spec[1, c] = dot(fwd[...], twice(csend[c]))
        return 0

    lax.fori_loop(0, chunks, transform_chunk, 0)

    def head_chunk(c, _):
        load(c, 1).wait()
        gate_copy(c).wait_recv()
        carry(c, 0, cold, grecv[c].astype(F32) * join0)
        spec[0, c] = dot(fwd[...], twice(cold[c]))
        return 0

    lax.fori_loop(0, chunks, head_chunk, 0)

    for d in range(1, side):
        table_copy(d).wait()
    for c in range(chunks):
        at = slice(c * CHUNK, (c + 1) * CHUNK)
        tsend[:, at] = pick_tiles(flip, at).astype(BF16)
    flip_copy().start()
    for c in range(chunks):
        at = slice(c * CHUNK, (c + 1) * CHUNK)
        rows_own[:, at] = pick_tiles(me, at).astype(BF16)

    half, quarter = TILE, TILE // 2

    def finish(c, i, prev, join):
        pre, pim = prev[:half] * join, prev[half:] * join
        cre, cim = spec[i, c, 0:half], spec[i, c, half:]
        gre = jnp.concatenate([cre[:quarter] - pim[:quarter], cre[quarter:] + pim[quarter:]], axis=0)
        gim = jnp.concatenate([cim[:quarter] + pre[:quarter], cim[quarter:] - pre[quarter:]], axis=0)
        hre, him = hspec[c, 0:half], hspec[c, half:]
        hi, lo = halves(jnp.concatenate([hre * gre - him * gim, hre * gim + him * gre], axis=0))
        both = dot(inv[...], hi)
        long_out = both[:TILE] + both[TILE:] + dot(inv[0:TILE], lo)
        base = TILE * i
        gate = s_buf[c, 3, pl.ds(base, TILE), :].astype(F32)
        hidden = (gate * long_out).astype(BF16)
        out[pl.ds(base, TILE), cols(c)] = hidden
        return hidden

    def project(c, hidden):
        return lax.dot_general(
            rows_own[:, cols(c)], hidden, (((1,), (1,)), ((), ())), preferred_element_type=F32
        )

    def share(i, projected):
        mine = projected[ROWS8 * i : ROWS8 * (i + 1)]
        rank = ROWS8 // 2
        delta = mine[rank:] - mine[:rank]
        psend[i] = jnp.concatenate([delta, jnp.zeros_like(delta)], axis=0)
        for d in range(1, n_chan):
            part_copy(i, d).start()

    def own_chunk(c, _):
        finish(c, 1, spec[0, c], join1)
        return 0

    lax.fori_loop(0, chunks, own_chunk, 0)
    flip_copy().wait()
    rows_own[...] = (rows_own[...].astype(F32) + trecv[...].astype(F32)).astype(BF16)
    zero = jnp.zeros((2 * ROWS8, TILE), F32)
    last = pl.ds(TILE, TILE)
    share(1, lax.fori_loop(0, chunks, lambda c, t: t + project(c, out[last, cols(c)]), zero))

    def border_chunk(c, t):
        border_copy(c).wait_recv()
        return t + project(c, finish(c, 0, dot(fwd[...], twice(crecv[c])), join0))

    share(0, lax.fori_loop(0, chunks, border_chunk, zero))

    row = lax.broadcasted_iota(jnp.int32, (ROWS8, TILE), 0)
    for i in (1, 0):
        s_of = seq_of(2 * me + i)
        owner = tenant[0]
        for s in range(1, SEQS):
            owner = jnp.where(s_of == s, tenant[s], owner)
        total = psend[i]
        for r in range(ROWS8 // 2):
            total += jnp.where(row == r, bias[r, owner], 0.0)
        for d in range(1, n_chan):
            part_copy(i, d).wait()
            total += precv[i, d - 1]
        blank = jnp.zeros_like(total)
        total = jnp.concatenate([total, blank] if i == 0 else [blank, total], axis=0)
        hi, lo = halves(jnp.concatenate([total, jnp.zeros((TILE - 2 * ROWS8, TILE), F32)], axis=0).T)
        spread = jnp.concatenate([hi[:, : 2 * ROWS8], lo[:, : 2 * ROWS8]], axis=1)
        rows = slice(TILE * i, TILE * (i + 1))

        def edit_chunk(c, _):
            change = dot(spread, twice(rows_own[:, cols(c)]))
            out[rows, cols(c)] = (out[rows, cols(c)].astype(F32) + change).astype(BF16)
            return 0

        lax.fori_loop(0, chunks, edit_chunk, 0)

    def drain(c, _):
        gate_copy(c).wait_send()
        border_copy(c).wait_send()
        return 0

    lax.fori_loop(0, chunks, drain, 0)


def on_device(n_seq, n_chan, streams, short_f, long_f, table, bias, tiles, tenant):
    rows, width = streams.shape[1:]
    chunks = width // CHUNK
    fwd, inv = transforms()
    vmem = pl.BlockSpec(memory_space=pltpu.VMEM)
    smem = pl.BlockSpec(memory_space=pltpu.SMEM)
    hbm = pl.BlockSpec(memory_space=pltpu.HBM)
    dma = pltpu.SemaphoreType.DMA
    return pl.pallas_call(
        functools.partial(main_kernel, n_seq, n_chan),
        out_shape=jax.ShapeDtypeStruct((rows, width), BF16),
        in_specs=[hbm, hbm, hbm, hbm, smem, smem, smem, hbm, hbm],
        out_specs=vmem,
        scratch_shapes=[
            pltpu.VMEM(short_f.shape, BF16),
            pltpu.VMEM(long_f.shape, BF16),
            pltpu.VMEM(table.shape, BF16),
            pltpu.VMEM(fwd.shape, BF16),
            pltpu.VMEM(inv.shape, BF16),
            pltpu.VMEM((2 * ROWS8, width), BF16),
            pltpu.VMEM((chunks, 5, rows, CHUNK), BF16),
            pltpu.VMEM((CHUNK // 128, LEAD + TILE, 128), F32),
            pltpu.VMEM((chunks, LEAD, CHUNK), BF16),
            pltpu.VMEM((chunks, LEAD, CHUNK), BF16),
            pltpu.VMEM((chunks, TILE, CHUNK), BF16),
            pltpu.VMEM((chunks, TILE, CHUNK), BF16),
            pltpu.VMEM((chunks, TILE, CHUNK), BF16),
            pltpu.VMEM((2, chunks, 2 * TILE, CHUNK), F32),
            pltpu.VMEM((chunks, 2 * TILE, CHUNK), F32),
            pltpu.VMEM((n_seq // 2 - 1, *table.shape), BF16),
            pltpu.VMEM((2 * ROWS8, width), BF16),
            pltpu.VMEM((2 * ROWS8, width), BF16),
            pltpu.VMEM((2, ROWS8, TILE), F32),
            pltpu.VMEM((2, n_chan - 1, ROWS8, TILE), F32),
            dma((2, chunks)),
            dma((5,)),
            dma((chunks,)),
            dma((chunks,)),
            dma((chunks,)),
            dma((chunks,)),
            dma((n_seq // 2,)),
            dma((n_seq // 2,)),
            dma((2, n_chan - 1)),
            dma((2, n_chan - 1)),
        ],
        compiler_params=pltpu.CompilerParams(
            collective_id=0, has_side_effects=True, vmem_limit_bytes=56 * 2**20
        ),
    )(streams, short_f, long_f, table, bias.T, tiles, tenant, jnp.asarray(fwd), jnp.asarray(inv))


def solution(mesh):
    in_specs = (
        P(None, "seq", "chan"),
        P(None, "chan"),
        P(None, "chan"),
        P("seq", None, "chan"),
        P(),
        P(),
        P(),
    )
    body = functools.partial(on_device, mesh.shape["seq"], mesh.shape["chan"])
    return jax.shard_map(
        body, mesh=mesh, in_specs=in_specs, out_specs=P("seq", "chan"), check_vma=False
    )
```

```python
import functools

import jax
import jax.numpy as jnp
import ml_dtypes
import numpy as np
from jax import lax
from jax.experimental import pallas as pl
from jax.experimental.pallas import tpu as pltpu
from jax.sharding import PartitionSpec as P

TILE = 128
SEQS = 4
ROWS8 = 8
CHUNK = 512
LEAD = 16
BF16 = jnp.bfloat16
F32 = jnp.float32


def split_np(a):
    hi = a.astype(ml_dtypes.bfloat16)
    lo = (a - hi.astype(np.float64)).astype(ml_dtypes.bfloat16)
    return hi, lo


def transforms():
    ks = np.concatenate([np.arange(0, TILE, 2), np.arange(1, TILE, 2)])
    angle = np.pi * np.outer(ks + 0.5, np.arange(TILE)) / TILE
    hi, lo = split_np(np.concatenate([np.cos(angle), -np.sin(angle)], axis=0))
    forward = np.concatenate([hi, lo], axis=1)
    back = np.concatenate([np.cos(angle).T, -np.sin(angle).T], axis=1) / TILE
    hi, lo = split_np(back)
    return forward, np.concatenate([hi, lo], axis=0)


def halves(x):
    hi = x.astype(BF16)
    return hi, (x - hi.astype(F32)).astype(BF16)


def dot(a, b):
    return jnp.dot(a, b, preferred_element_type=F32)


def main_kernel(
    n_seq, n_chan,
    streams, short_h, long_h, table_h, bias, tiles, tenant, fwd_h, inv_h,
    out,
    short_f, long_f, table, fwd, inv, rows_own,
    s_buf, gwin, gsend, grecv, csend, crecv, cold, spec, hspec, tcol, tsend, trecv, psend, precv,
    in_sem, side_sem, g_ss, g_rs, c_ss, c_rs, t_ss, t_rs, p_ss, p_rs,
):
    chunks = s_buf.shape[0]
    per = table.shape[0]
    side = n_seq // 2
    me = lax.axis_index("seq")
    z = lax.axis_index("chan")
    after = lax.rem(me + 1, n_seq)
    before = lax.rem(me + n_seq - 1, n_seq)

    flip = me + 2 - 4 * lax.rem(lax.div(me, 2), 2)
    place = lax.div(me, 4) * 2 + lax.rem(me, 2)

    def beside(d):
        at = lax.rem(place + d + side, side)
        return lax.div(at, 2) * 4 + lax.rem(lax.div(me, 2), 2) * 2 + lax.rem(at, 2)

    def peer(d):
        return lax.rem(z + d, n_chan)

    def cols(c):
        return pl.ds(pl.multiple_of(c * CHUNK, CHUNK), CHUNK)

    tail = pl.ds(TILE - LEAD, TILE + LEAD)
    head = pl.ds(0, TILE - LEAD)

    def load(c, part):
        rows = tail if part == 0 else head
        return pltpu.make_async_copy(
            streams.at[:, rows, cols(c)], s_buf.at[c, :, rows, :], in_sem.at[part, c]
        )

    sides = [
        pltpu.make_async_copy(src, dst, side_sem.at[k])
        for k, (src, dst) in enumerate(
            ((table_h, table), (short_h, short_f), (fwd_h, fwd), (long_h, long_f), (inv_h, inv))
        )
    ]
    sides[0].start()
    sides[1].start()
    for c in range(chunks):
        load(c, 0).start()
    for k in (2, 3, 4):
        sides[k].start()
    for c in range(chunks):
        load(c, 1).start()

    barrier = pltpu.get_barrier_semaphore()
    greeted = [{"seq": after}, {"seq": before}]
    greeted += [{"seq": beside(d)} for d in range(1, side)] + [{"seq": flip}]
    greeted += [{"chan": peer(d)} for d in range(1, n_chan)]
    for who in greeted:
        pl.semaphore_signal(barrier, inc=1, device_id=who, device_id_type=pl.DeviceIdType.MESH)

    def remote(src, dst, ss, rs, who):
        return pltpu.make_async_remote_copy(
            src_ref=src, dst_ref=dst, send_sem=ss, recv_sem=rs, device_id=who,
            device_id_type=pl.DeviceIdType.MESH,
        )

    def table_copy(d):
        return remote(table, tcol.at[d - 1], t_ss.at[d], t_rs.at[d], {"seq": beside(d)})

    def flip_copy():
        return remote(tsend, trecv, t_ss.at[0], t_rs.at[0], {"seq": flip})

    def gate_copy(c):
        return remote(gsend.at[c], grecv.at[c], g_ss.at[c], g_rs.at[c], {"seq": after})

    def border_copy(c):
        return remote(csend.at[c], crecv.at[c], c_ss.at[c], c_rs.at[c], {"seq": after})

    def part_copy(i, d):
        return remote(
            psend.at[i], precv.at[i, d - 1], p_ss.at[i, d - 1], p_rs.at[i, d - 1], {"chan": peer(d)}
        )

    ends = []
    for s in range(SEQS):
        ends.append(tiles[s] if s == 0 else ends[-1] + tiles[s])

    def seq_of(tile):
        return sum(jnp.where(e <= tile, 1, 0) for e in ends)

    def joined(tile):
        hits = sum(jnp.where(e == tile, 1, 0) for e in ends) + jnp.where(tile == 0, 1, 0)
        return jnp.where(hits > 0, 0.0, 1.0).astype(F32)

    join0, join1 = joined(2 * me), joined(2 * me + 1)

    def pick_tiles(who, at):
        owned = [(me, table)] + [(beside(-d), tcol.at[d - 1]) for d in range(1, side)]
        picked = []
        for i in range(2):
            s_of = seq_of(2 * who + i)
            wanted = tenant[0]
            for s in range(1, SEQS):
                wanted = jnp.where(s_of == s, tenant[s], wanted)
            total = jnp.zeros((ROWS8, CHUNK), F32)
            for owner, rows in owned:
                for k in range(per):
                    factor = jnp.where(wanted == per * owner + k, 1.0, 0.0).astype(F32)
                    total += factor * rows[k, :, at].astype(F32)
            picked.append(total)
        return jnp.concatenate(picked, axis=0)

    def carry(c, i, dst, lead):
        base = TILE * i
        for b in range(CHUNK // 128):
            gwin[b, 0:LEAD] = lead[:, 128 * b : 128 * (b + 1)]
        key = s_buf[c, 1, pl.ds(base, TILE), :].astype(F32)
        val = s_buf[c, 2, pl.ds(base, TILE), :].astype(F32)
        gated = (key * val).astype(BF16)
        if i == 1:
            gsend[c] = gated[TILE - LEAD :]
        for b in range(CHUNK // 128):
            gwin[b, LEAD:] = gated[:, 128 * b : 128 * (b + 1)].astype(F32)
        taps = short_f[:, cols(c)].astype(F32)
        for b in range(CHUNK // 128):
            at = slice(128 * b, 128 * (b + 1))
            total = jnp.zeros((TILE, 128), F32)
            for j in range(short_f.shape[0]):
                total += taps[j : j + 1, at] * gwin[b, LEAD - j : LEAD - j + TILE]
            gate = s_buf[c, 0, pl.ds(base, TILE), at].astype(F32)
            mixed = (gate * total).astype(BF16).astype(F32)
            key2 = s_buf[c, 4, pl.ds(base, TILE), at].astype(F32)
            dst[c, :, at] = (key2 * mixed).astype(BF16)

    def tail_chunk(c, _):
        load(c, 0).wait()
        near = pl.ds(TILE - LEAD, LEAD)
        lead = (s_buf[c, 1, near, :].astype(F32) * s_buf[c, 2, near, :].astype(F32)).astype(BF16)
        carry(c, 1, csend, lead.astype(F32) * join1)
        return 0

    sides[1].wait()
    lax.fori_loop(0, chunks, tail_chunk, 0)

    def twice(x):
        return jnp.concatenate([x, x], axis=0)

    def filter_chunk(c, _):
        hspec[c] = dot(fwd[...], twice(long_f[:, cols(c)]))
        return 0

    sides[0].wait()
    pl.semaphore_wait(barrier, len(greeted))
    for c in range(chunks):
        gate_copy(c).start()
    for d in range(1, side):
        table_copy(d).start()
    for c in range(chunks):
        border_copy(c).start()

    for k in (2, 3, 4):
        sides[k].wait()
    lax.fori_loop(0, chunks, filter_chunk, 0)

    def transform_chunk(c, _):
        spec[1, c] = dot(fwd[...], twice(csend[c]))
        return 0

    lax.fori_loop(0, chunks, transform_chunk, 0)

    def head_chunk(c, _):
        load(c, 1).wait()
        gate_copy(c).wait_recv()
        carry(c, 0, cold, grecv[c].astype(F32) * join0)
        spec[0, c] = dot(fwd[...], twice(cold[c]))
        return 0

    lax.fori_loop(0, chunks, head_chunk, 0)

    for d in range(1, side):
        table_copy(d).wait()
    for c in range(chunks):
        at = slice(c * CHUNK, (c + 1) * CHUNK)
        tsend[:, at] = pick_tiles(flip, at).astype(BF16)
    flip_copy().start()
    for c in range(chunks):
        at = slice(c * CHUNK, (c + 1) * CHUNK)
        rows_own[:, at] = pick_tiles(me, at).astype(BF16)

    half, quarter = TILE, TILE // 2

    def finish(c, i, prev, join):
        pre, pim = prev[:half] * join, prev[half:] * join
        cre, cim = spec[i, c, 0:half], spec[i, c, half:]
        gre = jnp.concatenate([cre[:quarter] - pim[:quarter], cre[quarter:] + pim[quarter:]], axis=0)
        gim = jnp.concatenate([cim[:quarter] + pre[:quarter], cim[quarter:] - pre[quarter:]], axis=0)
        hre, him = hspec[c, 0:half], hspec[c, half:]
        hi, lo = halves(jnp.concatenate([hre * gre - him * gim, hre * gim + him * gre], axis=0))
        both = dot(inv[...], hi)
        long_out = both[:TILE] + both[TILE:] + dot(inv[0:TILE], lo)
        base = TILE * i
        gate = s_buf[c, 3, pl.ds(base, TILE), :].astype(F32)
        hidden = (gate * long_out).astype(BF16)
        out[pl.ds(base, TILE), cols(c)] = hidden
        return hidden

    def project(c, hidden):
        return lax.dot_general(
            rows_own[:, cols(c)], hidden, (((1,), (1,)), ((), ())), preferred_element_type=F32
        )

    def share(i, projected):
        mine = projected[ROWS8 * i : ROWS8 * (i + 1)]
        rank = ROWS8 // 2
        delta = mine[rank:] - mine[:rank]
        psend[i] = jnp.concatenate([delta, jnp.zeros_like(delta)], axis=0)
        for d in range(1, n_chan):
            part_copy(i, d).start()

    def own_chunk(c, _):
        finish(c, 1, spec[0, c], join1)
        return 0

    lax.fori_loop(0, chunks, own_chunk, 0)
    flip_copy().wait()
    rows_own[...] = (rows_own[...].astype(F32) + trecv[...].astype(F32)).astype(BF16)
    zero = jnp.zeros((2 * ROWS8, TILE), F32)
    last = pl.ds(TILE, TILE)
    share(1, lax.fori_loop(0, chunks, lambda c, t: t + project(c, out[last, cols(c)]), zero))

    def border_chunk(c, t):
        border_copy(c).wait_recv()
        return t + project(c, finish(c, 0, dot(fwd[...], twice(crecv[c])), join0))

    share(0, lax.fori_loop(0, chunks, border_chunk, zero))

    row = lax.broadcasted_iota(jnp.int32, (ROWS8, TILE), 0)
    for i in (1, 0):
        s_of = seq_of(2 * me + i)
        owner = tenant[0]
        for s in range(1, SEQS):
            owner = jnp.where(s_of == s, tenant[s], owner)
        total = psend[i]
        for r in range(ROWS8 // 2):
            total += jnp.where(row == r, bias[r, owner], 0.0)
        for d in range(1, n_chan):
            part_copy(i, d).wait()
            total += precv[i, d - 1]
        blank = jnp.zeros_like(total)
        total = jnp.concatenate([total, blank] if i == 0 else [blank, total], axis=0)
        hi, lo = halves(jnp.concatenate([total, jnp.zeros((TILE - 2 * ROWS8, TILE), F32)], axis=0).T)
        spread = jnp.concatenate([hi[:, : 2 * ROWS8], lo[:, : 2 * ROWS8]], axis=1)
        rows = slice(TILE * i, TILE * (i + 1))

        def edit_chunk(c, _):
            change = dot(spread, twice(rows_own[:, cols(c)]))
            out[rows, cols(c)] = (out[rows, cols(c)].astype(F32) + change).astype(BF16)
            return 0

        lax.fori_loop(0, chunks, edit_chunk, 0)

    def drain(c, _):
        gate_copy(c).wait_send()
        border_copy(c).wait_send()
        return 0

    lax.fori_loop(0, chunks, drain, 0)


def on_device(n_seq, n_chan, streams, short_f, long_f, table, bias, tiles, tenant):
    rows, width = streams.shape[1:]
    chunks = width // CHUNK
    fwd, inv = transforms()
    vmem = pl.BlockSpec(memory_space=pltpu.VMEM)
    smem = pl.BlockSpec(memory_space=pltpu.SMEM)
    hbm = pl.BlockSpec(memory_space=pltpu.HBM)
    dma = pltpu.SemaphoreType.DMA
    return pl.pallas_call(
        functools.partial(main_kernel, n_seq, n_chan),
        out_shape=jax.ShapeDtypeStruct((rows, width), BF16),
        in_specs=[hbm, hbm, hbm, hbm, smem, smem, smem, hbm, hbm],
        out_specs=vmem,
        scratch_shapes=[
            pltpu.VMEM(short_f.shape, BF16),
            pltpu.VMEM(long_f.shape, BF16),
            pltpu.VMEM(table.shape, BF16),
            pltpu.VMEM(fwd.shape, BF16),
            pltpu.VMEM(inv.shape, BF16),
            pltpu.VMEM((2 * ROWS8, width), BF16),
            pltpu.VMEM((chunks, 5, rows, CHUNK), BF16),
            pltpu.VMEM((CHUNK // 128, LEAD + TILE, 128), F32),
            pltpu.VMEM((chunks, LEAD, CHUNK), BF16),
            pltpu.VMEM((chunks, LEAD, CHUNK), BF16),
            pltpu.VMEM((chunks, TILE, CHUNK), BF16),
            pltpu.VMEM((chunks, TILE, CHUNK), BF16),
            pltpu.VMEM((chunks, TILE, CHUNK), BF16),
            pltpu.VMEM((2, chunks, 2 * TILE, CHUNK), F32),
            pltpu.VMEM((chunks, 2 * TILE, CHUNK), F32),
            pltpu.VMEM((n_seq // 2 - 1, *table.shape), BF16),
            pltpu.VMEM((2 * ROWS8, width), BF16),
            pltpu.VMEM((2 * ROWS8, width), BF16),
            pltpu.VMEM((2, ROWS8, TILE), F32),
            pltpu.VMEM((2, n_chan - 1, ROWS8, TILE), F32),
            dma((2, chunks)),
            dma((5,)),
            dma((chunks,)),
            dma((chunks,)),
            dma((chunks,)),
            dma((chunks,)),
            dma((n_seq // 2,)),
            dma((n_seq // 2,)),
            dma((2, n_chan - 1)),
            dma((2, n_chan - 1)),
        ],
        compiler_params=pltpu.CompilerParams(
            collective_id=0, has_side_effects=True, vmem_limit_bytes=56 * 2**20
        ),
    )(streams, short_f, long_f, table, bias.T, tiles, tenant, jnp.asarray(fwd), jnp.asarray(inv))


def solution(mesh):
    in_specs = (
        P(None, "seq", "chan"),
        P(None, "chan"),
        P(None, "chan"),
        P("seq", None, "chan"),
        P(),
        P(),
        P(),
    )
    body = functools.partial(on_device, mesh.shape["seq"], mesh.shape["chan"])
    return jax.shard_map(
        body, mesh=mesh, in_specs=in_specs, out_specs=P("seq", "chan"), check_vma=False
    )
```
